32 devices in a mesh: groups: 2 (over x), particle: 16 (over z, y, core).
Axes of the slice: x: 2, y: 2, z: 4, core: 2. Of those that a mesh axis runs over, the one named last changes fastest.
Arguments:
- pool: bfloat16 [4096, 2, 8, 1024], P(('groups', 'particle')), parts along dimension 0, may hold values from -6 to 6
- page_table: int32 [2048, 2], P(('groups', 'particle')), parts along dimension 0, may hold values from 0 to 127, as said below
- lengths: int32 [2048], P('groups'), parts along dimension 0, may hold values from 1 to 15
- ancestors: int32 [2048], P('groups'), parts along dimension 0, may hold values from 0 to 1023, as said below
- new_q: bfloat16 [2048, 8192], P(('groups', 'particle')), parts along dimension 0, may hold values from -70 to 70
- new_kv: bfloat16 [2048, 2, 1024], P(('groups', 'particle')), parts along dimension 0, may hold values from -6 to 6
- score_weight: float32 [8192], replicated, may hold values from -3 to 3
Outputs:
- new_pool: bfloat16 [4096, 2, 8, 1024], P(('groups', 'particle')), parts along dimension 0
- attn_out: bfloat16 [2048, 8192], P(('groups', 'particle')), parts along dimension 0
- log_weights: float32 [2048], P(('groups', 'particle')), parts along dimension 0
The draws below stay inside these ranges and needn't reach their ends.
There are 2 independent parts, one for each index of `groups`. The reference program is written for one: setup_inputs(seed, part) draws one part's arguments, and reference() takes and returns one part's arrays. A program takes and returns all parts, laid end to end along the dimension named above; an argument that names none is the same for every part. Nothing has to cross between parts.
Inputs may be any that keep to these rules, and one draw needn't show every extreme that they name: page_table's rows of one device together name every slot 0 to 127 once. ancestors[n] belongs to the same prompt as n; among the 64 particles of one device at most 8 have their ancestors on any one device, and some device pair reaches 8.
All inputs are finite; a program needn't handle non-finite values.
Results may differ from the reference program's by a relative error of at most 0.0085.
Values may be sent and summed in bfloat16 or wider, within the bound.
A program may use at most 128 MiB of HBM per device.

```python
import jax
import jax.numpy as jnp
from jax import lax

HEADS = 64
KV_HEADS = 8
HEAD_DIM = 128
GROUP = 64
P_DEV = 64
PAGE = 8
PAGES = 2
Q_WIDTH = 8192
KV_WIDTH = 1024
CTX = 16
PARTICLES = 1024
PROMPTS = 16
STRIDE = 1
REACH = 16
CAP = 8


def draw_page_table(key, part):
    key = jax.random.fold_in(key, 3)
    devices = PARTICLES // P_DEV
    layouts = jax.vmap(lambda single: jax.random.permutation(single, P_DEV * PAGES))(jax.random.split(key, devices))
    return layouts.reshape(PARTICLES, PAGES).astype(jnp.int32)


def draw_ancestors(key, part):
    key = jax.random.fold_in(key, 7)
    devices = PARTICLES // P_DEV
    key_order, key_shift, key_member = jax.random.split(key, 3)
    row_order = jax.vmap(lambda single: jax.random.permutation(single, P_DEV))(jax.random.split(key_order, devices))
    shifted = jax.random.randint(key_shift, (devices, 1), 0, REACH)
    relative = (row_order // CAP + shifted) % REACH
    target = jnp.arange(devices, dtype=jnp.int32)[:, None]
    source = target % STRIDE + STRIDE * relative
    column = jnp.arange(P_DEV, dtype=jnp.int32)[None, :]
    members = max(1, P_DEV // PROMPTS)
    base_row = ((target - source) * P_DEV + column) % PROMPTS
    picked = jax.random.randint(key_member, (devices, P_DEV), 0, members)
    chosen = source * P_DEV + base_row + PROMPTS * picked
    return chosen.reshape(PARTICLES).astype(jnp.int32)


def draw_new_q(key, part):
    key = jax.random.fold_in(key, 11)
    key_base = jax.random.fold_in(key, 0)
    values = jax.random.normal(key_base, (PARTICLES, Q_WIDTH), dtype=jnp.float32)
    return jnp.clip(values, -70.0, 70.0).astype(jnp.bfloat16)


def draw_score_weight(key, part):
    key = jax.random.fold_in(key, 13)
    values = jnp.clip(jax.random.normal(key, (Q_WIDTH,), dtype=jnp.float32) * 0.1, -0.6, 0.6)
    return values.astype(jnp.float32)


def place_ends(result, rng, low, largest):
    spot = [jax.random.randint(jax.random.fold_in(rng, axis), (), 0, length) for axis, length in enumerate(result.shape)]
    widest = result.shape.index(max(result.shape))
    next_to = spot[:widest] + [(spot[widest] + 1) % result.shape[widest]] + spot[widest + 1:]
    return result.at[tuple(spot)].set(low).at[tuple(next_to)].set(largest)


def shard_levels(own_key, extent, shards, low, high):
    gain, own = 1.0, jax.random.fold_in(own_key, 6)
    for dim, shards_of in shards:
        draws = jnp.exp(jax.random.uniform(jax.random.fold_in(own, dim), (shards_of,), jnp.float32, low / len(shards), high / len(shards)))
        gain = gain * jnp.repeat(draws, extent[dim] // shards_of).reshape([-1 if axis == dim else 1 for axis in range(len(extent))])
    return gain


def noise(key, extent, scale, most, shards=(), held_as=jnp.bfloat16):
    result = jax.random.normal(key, extent, jnp.float32) * scale
    if len(shards) > 0:
        result = shard_levels(key, extent, shards, -0.22, 0.18) * result
    return jnp.clip(result, min=-most, max=most).astype(held_as)


def setup_inputs(seed: int = 0, part: int = 0) -> dict:
    arg_keys = jax.random.split(jax.random.key(seed), 8)
    part_splits = jax.random.split(jax.random.fold_in(arg_keys[7], part), 8)
    pool = noise(part_splits[0], (PARTICLES * PAGES, 2, PAGE, KV_WIDTH), 1.0, 6.0, ((0, 16),))
    page_table = draw_page_table(jax.random.fold_in(jax.random.fold_in(arg_keys[7], part), 71), part)
    lengths = place_ends(jax.random.randint(part_splits[2], (PARTICLES,), 1, CTX), jax.random.fold_in(part_splits[2], 1), 1, CTX - 1).astype(jnp.int32)
    ancestors = draw_ancestors(jax.random.fold_in(jax.random.fold_in(arg_keys[7], part), 71), part)
    new_q = draw_new_q(jax.random.fold_in(jax.random.fold_in(arg_keys[7], part), 71), part)
    new_kv = noise(part_splits[5], (PARTICLES, 2, KV_WIDTH), 1.0, 6.0, ((0, 16),))
    score_weight = draw_score_weight(jax.random.fold_in(arg_keys[7], 71), part)
    return dict(pool=pool, page_table=page_table, lengths=lengths, ancestors=ancestors, new_q=new_q, new_kv=new_kv, score_weight=score_weight)


def attend(query, held, length_now):
    rows = query.shape[0]
    key_rows = held[:, :, 0].reshape(rows, CTX, KV_HEADS, HEAD_DIM).astype(jnp.float32)
    value_rows = held[:, :, 1].reshape(rows, CTX, KV_HEADS, HEAD_DIM).astype(jnp.float32)
    grouped = query.reshape(rows, KV_HEADS, HEADS // KV_HEADS, HEAD_DIM).astype(jnp.float32)
    scores = jnp.einsum('pgrd,ptgd->pgrt', grouped, key_rows) * (HEAD_DIM ** -0.5)
    visible = jnp.arange(CTX, dtype=jnp.int32)[None, :] <= length_now[:, None]
    scores = jnp.where(visible[:, None, None, :], scores, -1e30)
    highest = jnp.max(scores, axis=3, keepdims=True)
    expo = jnp.exp(scores - highest)
    probs = (expo / jnp.sum(expo, axis=3, keepdims=True)).astype(jnp.bfloat16)
    mixed_heads = jnp.einsum('pgrt,ptgd->pgrd', probs.astype(jnp.float32), value_rows)
    return mixed_heads.reshape(rows, Q_WIDTH).astype(jnp.bfloat16)


def reference(pool, page_table, lengths, ancestors, new_q, new_kv, score_weight):
    owner_base = (jnp.arange(PARTICLES, dtype=jnp.int32) // P_DEV) * (P_DEV * PAGES)
    slots = owner_base[:, None] + page_table
    held_pages = pool[slots]
    inherited = held_pages[ancestors]
    length_now = lengths[ancestors]
    position = jnp.arange(CTX, dtype=jnp.int32).reshape(PAGES, PAGE)
    at_new = position[None] == length_now[:, None, None]
    descended = jnp.where(at_new[:, :, None, :, None], new_kv[:, None, :, None, :], inherited)
    new_pool = jnp.zeros_like(pool).at[slots.reshape(-1)].set(descended.reshape(PARTICLES * PAGES, 2, PAGE, KV_WIDTH))
    blocks = PARTICLES // P_DEV
    attn_out = lax.map(lambda group_args: attend(*group_args),
                       (new_q.reshape(blocks, P_DEV, Q_WIDTH),
                        descended.reshape((blocks, P_DEV) + descended.shape[1:]),
                        length_now.reshape(blocks, P_DEV))).reshape(PARTICLES, Q_WIDTH)
    reward = jnp.sum(attn_out.astype(jnp.float32) * score_weight[None, :], axis=1)
    table = reward.reshape(GROUP, PROMPTS)
    highest = jnp.max(table, axis=0)
    summed = jnp.sum(jnp.exp(table - highest[None, :]), axis=0)
    log_weights = (table - (highest + jnp.log(summed))[None, :]).reshape(PARTICLES)
    return new_pool, attn_out, log_weights
```

```python
import functools

import jax
import jax.numpy as jnp
from jax import lax
from jax.experimental import pallas as pl
from jax.experimental.pallas import tpu as pltpu
from jax.sharding import PartitionSpec as P

HEADS = 64
KV_HEADS = 8
HEAD_DIM = 128
GROUP = 64
BATCH = 8


def pack_kernel(slots, pages, row_ref, table_ref, pool_ref, out_ref, sem):
    def step(j, carry):
        row = row_ref[j]
        for i in range(pages):
            slot = table_ref[row * pages + i]
            pltpu.make_async_copy(pool_ref.at[slot], out_ref.at[j, i], sem).start()
        return carry

    lax.fori_loop(0, slots, step, 0, unroll=4)
    pltpu.make_async_copy(out_ref, out_ref, sem).wait()


def pack(pool, table, source_row, pages):
    slots = source_row.shape[0]
    return pl.pallas_call(
        functools.partial(pack_kernel, slots, pages),
        out_shape=jax.ShapeDtypeStruct((slots, pages) + pool.shape[1:], pool.dtype),
        in_specs=[
            pl.BlockSpec(memory_space=pltpu.SMEM),
            pl.BlockSpec(memory_space=pltpu.SMEM),
            pl.BlockSpec(memory_space=pltpu.VMEM),
        ],
        out_specs=pl.BlockSpec(memory_space=pl.ANY),
        scratch_shapes=[pltpu.SemaphoreType.DMA],
        compiler_params=pltpu.CompilerParams(vmem_limit_bytes=24 << 20),
        name="pack",
    )(source_row, table, pool)


def attend_kernel(
    rows, pages, arrive_ref, table_ref, len_ref,
    held_ref, q_ref, kv_ref, weight_ref,
    pool_ref, attn_ref, part_ref,
    buf, in_sem, out_sem,
):
    page_len = buf.shape[3]
    width = buf.shape[4]
    ctx = pages * page_len

    def fetch(p, carry):
        pltpu.make_async_copy(held_ref.at[arrive_ref[p]], buf.at[p], in_sem.at[p]).start()
        return carry

    lax.fori_loop(0, rows, fetch, 0, unroll=4)

    cols = KV_HEADS * ctx
    head = lax.broadcasted_iota(jnp.int32, (HEADS, cols), 0) // (HEADS // KV_HEADS)
    col = lax.broadcasted_iota(jnp.int32, (HEADS, cols), 1)
    place = jnp.where(head == col // ctx, col % ctx, ctx)
    row = lax.broadcasted_iota(jnp.int32, (page_len, width), 0)

    def step(b, carry):
        p0 = pl.multiple_of(b * BATCH, BATCH)
        fresh = kv_ref[pl.ds(p0, BATCH), :]
        scores = []
        values = []
        for r in range(BATCH):
            p = p0 + r
            pltpu.make_async_copy(held_ref.at[0], buf.at[p], in_sem.at[p]).wait()
            length = len_ref[p]
            cache = []
            for s in range(2):
                new_row = fresh[r:r + 1, s * width:(s + 1) * width]
                now = []
                for i in range(pages):
                    old = buf[p, i, s].astype(jnp.float32)
                    made = jnp.where(row + i * page_len == length, new_row, old)
                    buf[p, i, s] = made.astype(buf.dtype)
                    now.append(made)
                cache.append(jnp.concatenate(
                    [now[i][:, g * HEAD_DIM:(g + 1) * HEAD_DIM] for g in range(KV_HEADS) for i in range(pages)],
                    axis=0,
                ).astype(jnp.bfloat16))
            for i in range(pages):
                slot = table_ref[p * pages + i]
                pltpu.make_async_copy(buf.at[p, i], pool_ref.at[slot], out_sem).start()
            logits = lax.dot_general(
                q_ref[p], cache[0], (((1,), (1,)), ((), ())), preferred_element_type=jnp.float32
            )
            scores.append(jnp.where(place <= length, logits * HEAD_DIM ** (-0.5), -1e30))
            values.append(cache[1])
        weight = weight_ref[...]
        totals = []
        for r in range(BATCH):
            high = jnp.max(scores[r], axis=1, keepdims=True)
            expo = jnp.exp(scores[r] - high)
            probs = (expo / jnp.sum(expo, axis=1, keepdims=True)).astype(jnp.bfloat16)
            mixed = jnp.dot(probs, values[r], preferred_element_type=jnp.float32).astype(attn_ref.dtype)
            attn_ref[p0 + r] = mixed
            totals.append(jnp.sum(mixed.astype(jnp.float32) * weight, axis=0, keepdims=True))
        part_ref[pl.ds(p0, BATCH), :] = jnp.concatenate(totals, axis=0)
        return carry

    lax.fori_loop(0, rows // BATCH, step, 0)
    pltpu.make_async_copy(buf, buf, out_sem).wait()


def attend(held, arrive, table, length_now, query, fresh, weight, pool):
    rows = query.shape[0]
    pages = held.shape[1]
    return pl.pallas_call(
        functools.partial(attend_kernel, rows, pages),
        out_shape=(
            jax.ShapeDtypeStruct(pool.shape, pool.dtype),
            jax.ShapeDtypeStruct(query.shape, jnp.bfloat16),
            jax.ShapeDtypeStruct((rows, HEAD_DIM), jnp.float32),
        ),
        in_specs=[pl.BlockSpec(memory_space=pltpu.SMEM)] * 3
        + [pl.BlockSpec(memory_space=pl.ANY)]
        + [pl.BlockSpec(memory_space=pltpu.VMEM)] * 3,
        out_specs=(
            pl.BlockSpec(memory_space=pl.ANY),
            pl.BlockSpec(memory_space=pltpu.VMEM),
            pl.BlockSpec(memory_space=pltpu.VMEM),
        ),
        scratch_shapes=[
            pltpu.VMEM((rows,) + held.shape[1:], held.dtype),
            pltpu.SemaphoreType.DMA((rows,)),
            pltpu.SemaphoreType.DMA,
        ],
        compiler_params=pltpu.CompilerParams(vmem_limit_bytes=32 << 20),
        name="attend",
    )(arrive, table, length_now, held, query, fresh, weight)


def spread_kernel(devices, mine_ref, all_ref, landed, send_sem, recv_sem):
    me = lax.axis_index("particle")
    barrier = pltpu.get_barrier_semaphore()

    def greet(k, carry):
        pl.semaphore_signal(
            barrier, inc=1, device_id={"particle": lax.rem(me + k, devices)},
            device_id_type=pl.DeviceIdType.MESH,
        )
        return carry

    lax.fori_loop(1, devices, greet, 0)
    pl.semaphore_wait(barrier, devices - 1)

    def copy_to(k):
        return pltpu.make_async_remote_copy(
            src_ref=mine_ref,
            dst_ref=landed.at[k],
            send_sem=send_sem.at[k],
            recv_sem=recv_sem.at[k],
            device_id={"particle": lax.rem(me + k, devices)},
            device_id_type=pl.DeviceIdType.MESH,
        )

    def send(k, carry):
        copy_to(k).start()
        return carry

    def finish(k, carry):
        copy_to(k).wait()
        return carry

    lax.fori_loop(1, devices, send, 0)
    landed[0] = mine_ref[...]
    lax.fori_loop(1, devices, finish, 0)
    all_ref[...] = landed[...]


def spread(mine, devices):
    return pl.pallas_call(
        functools.partial(spread_kernel, devices),
        out_shape=jax.ShapeDtypeStruct((devices,) + mine.shape, mine.dtype),
        in_specs=[pl.BlockSpec(memory_space=pltpu.VMEM)],
        out_specs=pl.BlockSpec(memory_space=pltpu.VMEM),
        scratch_shapes=[
            pltpu.VMEM((devices,) + mine.shape, mine.dtype),
            pltpu.SemaphoreType.DMA((devices,)),
            pltpu.SemaphoreType.DMA((devices,)),
        ],
        compiler_params=pltpu.CompilerParams(collective_id=0, has_side_effects=True),
        name="spread",
    )(mine)


def local(pool, page_table, lengths, ancestors, new_q, new_kv, score_weight):
    devices = lax.axis_size("particle")
    self_index = lax.axis_index("particle")
    per_device = new_q.shape[0]
    page_count = page_table.shape[1]
    prompts = devices * per_device // GROUP
    stride = max(1, prompts // per_device)
    reach_size = devices // stride
    capacity = 2 * per_device // reach_size
    table = page_table.reshape(-1)
    anc_all = ancestors.reshape(devices, per_device)
    anc_dev = anc_all // per_device
    row_order = jnp.arange(per_device, dtype=jnp.int32)
    my_ancestors = lax.dynamic_slice_in_dim(anc_all, self_index, 1, 0)[0]
    my_sources = my_ancestors // per_device
    from_self = anc_dev == self_index
    slot_rank = jnp.cumsum(from_self.astype(jnp.int32), axis=1) - 1
    picked = from_self[:, None, :] & (
        slot_rank[:, None, :] == jnp.arange(capacity, dtype=jnp.int32)[None, :, None]
    )
    source_row = jnp.sum(jnp.where(picked, anc_all[:, None, :] % per_device, 0), axis=2)
    outgoing = pack(pool, table, source_row.reshape(-1), page_count)
    outgoing = outgoing.reshape((devices, capacity) + outgoing.shape[1:])
    incoming = lax.all_to_all(outgoing, "particle", split_axis=0, concat_axis=0, tiled=True)
    incoming = incoming.reshape((devices * capacity,) + incoming.shape[2:])
    earlier = (my_sources[None, :] == my_sources[:, None]) & (
        row_order[None, :] < row_order[:, None]
    )
    arrive_slot = my_sources * capacity + jnp.sum(earlier.astype(jnp.int32), axis=1)
    length_now = lengths[my_ancestors]
    new_pool, attn_out, partial_sums = attend(
        incoming, arrive_slot, table, length_now,
        new_q.reshape(per_device, HEADS, HEAD_DIM),
        new_kv.astype(jnp.float32).reshape(per_device, -1),
        score_weight.reshape(HEADS, HEAD_DIM), pool,
    )
    attn_out = attn_out.reshape(new_q.shape)
    reward = jnp.sum(partial_sums, axis=1)
    mine = jnp.broadcast_to(reward[None, :], (8, per_device))
    mine = jnp.pad(mine, ((0, 0), (0, (-per_device) % 128)))
    landed = spread(mine, devices)[:, 0, :per_device]
    owner = (self_index - jnp.arange(devices, dtype=jnp.int32)) % devices
    landed_prompt = (owner[:, None] * per_device + row_order[None, :]) % prompts
    my_prompt = (self_index * per_device + row_order) % prompts
    member = landed_prompt.reshape(-1)[None, :] == my_prompt[:, None]
    rewards = landed.reshape(-1)[None, :]
    highest = jnp.max(jnp.where(member, rewards, -jnp.inf), axis=1)
    summed = jnp.sum(jnp.exp(jnp.where(member, rewards - highest[:, None], -jnp.inf)), axis=1)
    log_weights = reward - (highest + jnp.log(summed))
    return (new_pool, attn_out, log_weights)


def solution(mesh):
    in_specs = (
        P(("groups", "particle"), None, None, None),
        P(("groups", "particle"), None),
        P("groups"),
        P("groups"),
        P(("groups", "particle"), None),
        P(("groups", "particle"), None, None),
        P(),
    )
    out_specs = (
        P(("groups", "particle"), None, None, None),
        P(("groups", "particle"), None),
        P(("groups", "particle")),
    )
    return jax.shard_map(local, mesh=mesh, in_specs=in_specs, out_specs=out_specs, check_vma=False)
```

```python
import functools

import jax
import jax.numpy as jnp
from jax import lax
from jax.experimental import pallas as pl
from jax.experimental.pallas import tpu as pltpu
from jax.sharding import PartitionSpec as P

HEADS = 64
KV_HEADS = 8
HEAD_DIM = 128
GROUP = 64
BATCH = 8


def exchange_kernel(
    devices, capacity, pages, row_ref, table_ref, pool_ref, held_ref,
    stage, send_sem, recv_sem, own_sem,
):
    me = lax.axis_index("particle")
    barrier = pltpu.get_barrier_semaphore()

    def greet(k, carry):
        pl.semaphore_signal(
            barrier, inc=1, device_id={"particle": lax.rem(me + k, devices)},
            device_id_type=pl.DeviceIdType.MESH,
        )
        return carry

    lax.fori_loop(1, devices, greet, 0)

    def fill(k):
        base = lax.rem(me + k, devices) * capacity
        for c in range(capacity):
            row = row_ref[base + c]
            for i in range(pages):
                stage[k, c, i] = pool_ref[table_ref[row * pages + i]]

    def copy_to(k):
        return pltpu.make_async_remote_copy(
            src_ref=stage.at[k],
            dst_ref=held_ref.at[me],
            send_sem=send_sem.at[k],
            recv_sem=recv_sem.at[k],
            device_id={"particle": lax.rem(me + k, devices)},
            device_id_type=pl.DeviceIdType.MESH,
        )

    def send(i, carry):
        half = i // 2
        odd = half % 2
        step = (half + 1) // 2
        far = devices // 2 + step - 2 * step * odd
        near = (1 - odd) * (devices - 1 - half // 2) + odd * (1 + half // 2)
        k = far + (i % 2) * (near - far)
        fill(k)
        copy_to(k).start()
        return carry

    def finish(k, carry):
        source = lax.rem(me + devices - k, devices)
        pltpu.make_async_remote_copy(
            src_ref=stage.at[k],
            dst_ref=held_ref.at[source],
            send_sem=send_sem.at[k],
            recv_sem=recv_sem.at[k],
            device_id={"particle": lax.rem(me + k, devices)},
            device_id_type=pl.DeviceIdType.MESH,
        ).wait()
        return carry

    pl.semaphore_wait(barrier, devices - 1)
    lax.fori_loop(0, devices - 1, send, 0)
    fill(0)
    own = pltpu.make_async_copy(stage.at[0], held_ref.at[me], own_sem)
    own.start()
    lax.fori_loop(1, devices, finish, 0)
    own.wait()


def exchange(pool, table, source_row, pages):
    devices, capacity = source_row.shape
    block = (capacity, pages) + pool.shape[1:]
    return pl.pallas_call(
        functools.partial(exchange_kernel, devices, capacity, pages),
        out_shape=jax.ShapeDtypeStruct((devices,) + block, pool.dtype),
        in_specs=[
            pl.BlockSpec(memory_space=pltpu.SMEM),
            pl.BlockSpec(memory_space=pltpu.SMEM),
            pl.BlockSpec(memory_space=pltpu.VMEM),
        ],
        out_specs=pl.BlockSpec(memory_space=pl.ANY),
        scratch_shapes=[
            pltpu.VMEM((devices,) + block, pool.dtype),
            pltpu.SemaphoreType.DMA((devices,)),
            pltpu.SemaphoreType.DMA((devices,)),
            pltpu.SemaphoreType.DMA,
        ],
        compiler_params=pltpu.CompilerParams(
            collective_id=1, has_side_effects=True, vmem_limit_bytes=40 << 20
        ),
        name="exchange",
    )(source_row.reshape(-1), table, pool)


def attend_kernel(
    rows, pages, arrive_ref, table_ref, len_ref,
    held_ref, q_ref, kv_ref, weight_ref,
    pool_ref, attn_ref, part_ref,
    buf, in_sem, out_sem,
):
    page_len = buf.shape[3]
    width = buf.shape[4]
    ctx = pages * page_len

    def fetch(p, carry):
        pltpu.make_async_copy(held_ref.at[arrive_ref[p]], buf.at[p], in_sem.at[p]).start()
        return carry

    lax.fori_loop(0, rows, fetch, 0, unroll=4)

    cols = KV_HEADS * ctx
    head = lax.broadcasted_iota(jnp.int32, (HEADS, cols), 0) // (HEADS // KV_HEADS)
    col = lax.broadcasted_iota(jnp.int32, (HEADS, cols), 1)
    place = jnp.where(head == col // ctx, col % ctx, ctx)
    row = lax.broadcasted_iota(jnp.int32, (page_len, width), 0)

    def step(b, carry):
        p0 = pl.multiple_of(b * BATCH, BATCH)
        fresh = kv_ref[pl.ds(p0, BATCH), :]
        scores = []
        values = []
        for r in range(BATCH):
            p = p0 + r
            pltpu.make_async_copy(held_ref.at[0], buf.at[p], in_sem.at[p]).wait()
            length = len_ref[p]
            cache = []
            for s in range(2):
                new_row = fresh[r:r + 1, s * width:(s + 1) * width]
                now = []
                for i in range(pages):
                    old = buf[p, i, s].astype(jnp.float32)
                    made = jnp.where(row + i * page_len == length, new_row, old)
                    buf[p, i, s] = made.astype(buf.dtype)
                    now.append(made)
                cache.append(jnp.concatenate(
                    [now[i][:, g * HEAD_DIM:(g + 1) * HEAD_DIM] for g in range(KV_HEADS) for i in range(pages)],
                    axis=0,
                ).astype(jnp.bfloat16))
            for i in range(pages):
                slot = table_ref[p * pages + i]
                pltpu.make_async_copy(buf.at[p, i], pool_ref.at[slot], out_sem).start()
            logits = lax.dot_general(
                q_ref[p], cache[0], (((1,), (1,)), ((), ())), preferred_element_type=jnp.float32
            )
            scores.append(jnp.where(place <= length, logits * HEAD_DIM ** (-0.5), -1e30))
            values.append(cache[1])
        weight = weight_ref[...]
        totals = []
        for r in range(BATCH):
            high = jnp.max(scores[r], axis=1, keepdims=True)
            expo = jnp.exp(scores[r] - high)
            probs = (expo / jnp.sum(expo, axis=1, keepdims=True)).astype(jnp.bfloat16)
            mixed = jnp.dot(probs, values[r], preferred_element_type=jnp.float32).astype(attn_ref.dtype)
            attn_ref[p0 + r] = mixed
            totals.append(jnp.sum(mixed.astype(jnp.float32) * weight, axis=0, keepdims=True))
        part_ref[pl.ds(p0, BATCH), :] = jnp.concatenate(totals, axis=0)
        return carry

    lax.fori_loop(0, rows // BATCH, step, 0)
    pltpu.make_async_copy(buf, buf, out_sem).wait()


def attend(held, arrive, table, length_now, query, fresh, weight, pool):
    rows = query.shape[0]
    pages = held.shape[1]
    return pl.pallas_call(
        functools.partial(attend_kernel, rows, pages),
        out_shape=(
            jax.ShapeDtypeStruct(pool.shape, pool.dtype),
            jax.ShapeDtypeStruct(query.shape, jnp.bfloat16),
            jax.ShapeDtypeStruct((rows, HEAD_DIM), jnp.float32),
        ),
        in_specs=[pl.BlockSpec(memory_space=pltpu.SMEM)] * 3
        + [pl.BlockSpec(memory_space=pl.ANY)]
        + [pl.BlockSpec(memory_space=pltpu.VMEM)] * 3,
        out_specs=(
            pl.BlockSpec(memory_space=pl.ANY),
            pl.BlockSpec(memory_space=pltpu.VMEM),
            pl.BlockSpec(memory_space=pltpu.VMEM),
        ),
        scratch_shapes=[
            pltpu.VMEM((rows,) + held.shape[1:], held.dtype),
            pltpu.SemaphoreType.DMA((rows,)),
            pltpu.SemaphoreType.DMA,
        ],
        compiler_params=pltpu.CompilerParams(vmem_limit_bytes=32 << 20),
        name="attend",
    )(arrive, table, length_now, held, query, fresh, weight)


def spread_kernel(devices, mine_ref, all_ref, landed, send_sem, recv_sem):
    me = lax.axis_index("particle")
    barrier = pltpu.get_barrier_semaphore()

    def greet(k, carry):
        pl.semaphore_signal(
            barrier, inc=1, device_id={"particle": lax.rem(me + k, devices)},
            device_id_type=pl.DeviceIdType.MESH,
        )
        return carry

    lax.fori_loop(1, devices, greet, 0)
    pl.semaphore_wait(barrier, devices - 1)

    def copy_to(k):
        return pltpu.make_async_remote_copy(
            src_ref=mine_ref,
            dst_ref=landed.at[k],
            send_sem=send_sem.at[k],
            recv_sem=recv_sem.at[k],
            device_id={"particle": lax.rem(me + k, devices)},
            device_id_type=pl.DeviceIdType.MESH,
        )

    def send(k, carry):
        copy_to(k).start()
        return carry

    def finish(k, carry):
        copy_to(k).wait()
        return carry

    lax.fori_loop(1, devices, send, 0)
    landed[0] = mine_ref[...]
    lax.fori_loop(1, devices, finish, 0)
    all_ref[...] = landed[...]


def spread(mine, devices):
    return pl.pallas_call(
        functools.partial(spread_kernel, devices),
        out_shape=jax.ShapeDtypeStruct((devices,) + mine.shape, mine.dtype),
        in_specs=[pl.BlockSpec(memory_space=pltpu.VMEM)],
        out_specs=pl.BlockSpec(memory_space=pltpu.VMEM),
        scratch_shapes=[
            pltpu.VMEM((devices,) + mine.shape, mine.dtype),
            pltpu.SemaphoreType.DMA((devices,)),
            pltpu.SemaphoreType.DMA((devices,)),
        ],
        compiler_params=pltpu.CompilerParams(collective_id=0, has_side_effects=True),
        name="spread",
    )(mine)


def local(pool, page_table, lengths, ancestors, new_q, new_kv, score_weight):
    devices = lax.axis_size("particle")
    self_index = lax.axis_index("particle")
    per_device = new_q.shape[0]
    page_count = page_table.shape[1]
    prompts = devices * per_device // GROUP
    stride = max(1, prompts // per_device)
    reach_size = devices // stride
    capacity = 2 * per_device // reach_size
    table = page_table.reshape(-1)
    anc_all = ancestors.reshape(devices, per_device)
    anc_dev = anc_all // per_device
    row_order = jnp.arange(per_device, dtype=jnp.int32)
    my_ancestors = lax.dynamic_slice_in_dim(anc_all, self_index, 1, 0)[0]
    my_sources = my_ancestors // per_device
    from_self = anc_dev == self_index
    slot_rank = jnp.cumsum(from_self.astype(jnp.int32), axis=1) - 1
    picked = from_self[:, None, :] & (
        slot_rank[:, None, :] == jnp.arange(capacity, dtype=jnp.int32)[None, :, None]
    )
    source_row = jnp.sum(jnp.where(picked, anc_all[:, None, :] % per_device, 0), axis=2)
    incoming = exchange(pool, table, source_row, page_count)
    incoming = incoming.reshape((devices * capacity,) + incoming.shape[2:])
    earlier = (my_sources[None, :] == my_sources[:, None]) & (
        row_order[None, :] < row_order[:, None]
    )
    arrive_slot = my_sources * capacity + jnp.sum(earlier.astype(jnp.int32), axis=1)
    length_now = lengths[my_ancestors]
    new_pool, attn_out, partial_sums = attend(
        incoming, arrive_slot, table, length_now,
        new_q.reshape(per_device, HEADS, HEAD_DIM),
        new_kv.astype(jnp.float32).reshape(per_device, -1),
        score_weight.reshape(HEADS, HEAD_DIM), pool,
    )
    attn_out = attn_out.reshape(new_q.shape)
    reward = jnp.sum(partial_sums, axis=1)
    mine = jnp.broadcast_to(reward[None, :], (8, per_device))
    mine = jnp.pad(mine, ((0, 0), (0, (-per_device) % 128)))
    landed = spread(mine, devices)[:, 0, :per_device]
    owner = (self_index - jnp.arange(devices, dtype=jnp.int32)) % devices
    landed_prompt = (owner[:, None] * per_device + row_order[None, :]) % prompts
    my_prompt = (self_index * per_device + row_order) % prompts
    member = landed_prompt.reshape(-1)[None, :] == my_prompt[:, None]
    rewards = landed.reshape(-1)[None, :]
    highest = jnp.max(jnp.where(member, rewards, -jnp.inf), axis=1)
    summed = jnp.sum(jnp.exp(jnp.where(member, rewards - highest[:, None], -jnp.inf)), axis=1)
    log_weights = reward - (highest + jnp.log(summed))
    return (new_pool, attn_out, log_weights)


def solution(mesh):
    in_specs = (
        P(("groups", "particle"), None, None, None),
        P(("groups", "particle"), None),
        P("groups"),
        P("groups"),
        P(("groups", "particle"), None),
        P(("groups", "particle"), None, None),
        P(),
    )
    out_specs = (
        P(("groups", "particle"), None, None, None),
        P(("groups", "particle"), None),
        P(("groups", "particle")),
    )
    return jax.shard_map(local, mesh=mesh, in_specs=in_specs, out_specs=out_specs, check_vma=False)
```

```python
import functools

import jax
import jax.numpy as jnp
from jax import lax
from jax.experimental import pallas as pl
from jax.experimental.pallas import tpu as pltpu
from jax.sharding import PartitionSpec as P

HEADS = 64
KV_HEADS = 8
HEAD_DIM = 128
GROUP = 64
BATCH = 16


def exchange_kernel(
    devices, capacity, pages, row_ref, table_ref, pool_ref, held_ref,
    stage, send_sem, recv_sem, own_sem,
):
    me = lax.axis_index("particle")
    barrier = pltpu.get_barrier_semaphore()

    def greet(k, carry):
        pl.semaphore_signal(
            barrier, inc=1, device_id={"particle": lax.rem(me + k, devices)},
            device_id_type=pl.DeviceIdType.MESH,
        )
        return carry

    lax.fori_loop(1, devices, greet, 0)

    def fill(k):
        base = lax.rem(me + k, devices) * capacity
        for c in range(capacity):
            row = row_ref[base + c]
            for i in range(pages):
                stage[k, c, i] = pool_ref[table_ref[row * pages + i]]

    def copy_to(k):
        return pltpu.make_async_remote_copy(
            src_ref=stage.at[k],
            dst_ref=held_ref.at[me],
            send_sem=send_sem.at[k],
            recv_sem=recv_sem.at[k],
            device_id={"particle": lax.rem(me + k, devices)},
            device_id_type=pl.DeviceIdType.MESH,
        )

    def send(i, carry):
        half = i // 2
        odd = half % 2
        step = (half + 1) // 2
        far = devices // 2 + step - 2 * step * odd
        near = (1 - odd) * (devices - 1 - half // 2) + odd * (1 + half // 2)
        k = far + (i % 2) * (near - far)
        fill(k)
        copy_to(k).start()
        return carry

    def finish(k, carry):
        source = lax.rem(me + devices - k, devices)
        pltpu.make_async_remote_copy(
            src_ref=stage.at[k],
            dst_ref=held_ref.at[source],
            send_sem=send_sem.at[k],
            recv_sem=recv_sem.at[k],
            device_id={"particle": lax.rem(me + k, devices)},
            device_id_type=pl.DeviceIdType.MESH,
        ).wait()
        return carry

    pl.semaphore_wait(barrier, devices - 1)
    lax.fori_loop(0, devices - 1, send, 0)
    fill(0)
    own = pltpu.make_async_copy(stage.at[0], held_ref.at[me], own_sem)
    own.start()
    lax.fori_loop(1, devices, finish, 0)
    own.wait()


def exchange(pool, table, source_row, pages):
    devices, capacity = source_row.shape
    block = (capacity, pages) + pool.shape[1:]
    return pl.pallas_call(
        functools.partial(exchange_kernel, devices, capacity, pages),
        out_shape=jax.ShapeDtypeStruct((devices,) + block, pool.dtype),
        in_specs=[
            pl.BlockSpec(memory_space=pltpu.SMEM),
            pl.BlockSpec(memory_space=pltpu.SMEM),
            pl.BlockSpec(memory_space=pltpu.VMEM),
        ],
        out_specs=pl.BlockSpec(memory_space=pltpu.HBM),
        scratch_shapes=[
            pltpu.VMEM((devices,) + block, pool.dtype),
            pltpu.SemaphoreType.DMA((devices,)),
            pltpu.SemaphoreType.DMA((devices,)),
            pltpu.SemaphoreType.DMA,
        ],
        compiler_params=pltpu.CompilerParams(
            collective_id=1, has_side_effects=True, vmem_limit_bytes=48 << 20
        ),
        name="exchange",
    )(source_row.reshape(-1), table, pool)


def attend_kernel(
    rows, pages, arrive_ref, table_ref, len_ref,
    held_ref, q_ref, kv_ref, weight_ref,
    pool_ref, attn_ref, part_ref,
    buf, in_sem, out_sem,
):
    page_len = buf.shape[3]
    width = buf.shape[4]
    ctx = pages * page_len

    def fetch(p, carry):
        pltpu.make_async_copy(held_ref.at[arrive_ref[p]], buf.at[p], in_sem.at[p]).start()
        return carry

    lax.fori_loop(0, rows, fetch, 0, unroll=4)

    cols = KV_HEADS * ctx
    head = lax.broadcasted_iota(jnp.int32, (HEADS, cols), 0) // (HEADS // KV_HEADS)
    col = lax.broadcasted_iota(jnp.int32, (HEADS, cols), 1)
    place = jnp.where(head == col // ctx, col % ctx, ctx)
    row = lax.broadcasted_iota(jnp.int32, (page_len, width), 0)

    def step(b, carry):
        p0 = pl.multiple_of(b * BATCH, BATCH)
        fresh = kv_ref[pl.ds(p0, BATCH), :]
        scores = []
        values = []
        for r in range(BATCH):
            p = p0 + r
            pltpu.make_async_copy(held_ref.at[0], buf.at[p], in_sem.at[p]).wait()
            length = len_ref[p]
            cache = []
            for s in range(2):
                new_row = fresh[r:r + 1, s * width:(s + 1) * width]
                now = []
                for i in range(pages):
                    old = buf[p, i, s].astype(jnp.float32)
                    made = jnp.where(row + i * page_len == length, new_row, old)
                    buf[p, i, s] = made.astype(buf.dtype)
                    now.append(made)
                cache.append(jnp.concatenate(
                    [now[i][:, g * HEAD_DIM:(g + 1) * HEAD_DIM] for g in range(KV_HEADS) for i in range(pages)],
                    axis=0,
                ).astype(jnp.bfloat16))
            for i in range(pages):
                slot = table_ref[p * pages + i]
                pltpu.make_async_copy(buf.at[p, i], pool_ref.at[slot], out_sem).start()
            logits = lax.dot_general(
                q_ref[p], cache[0], (((1,), (1,)), ((), ())), preferred_element_type=jnp.float32
            )
            scores.append(jnp.where(place <= length, logits * HEAD_DIM ** (-0.5), -1e30))
            values.append(cache[1])
        weight = weight_ref[...]
        totals = []
        for r in range(BATCH):
            high = jnp.max(scores[r], axis=1, keepdims=True)
            expo = jnp.exp(scores[r] - high)
            probs = (expo / jnp.sum(expo, axis=1, keepdims=True)).astype(jnp.bfloat16)
            mixed = jnp.dot(probs, values[r], preferred_element_type=jnp.float32).astype(attn_ref.dtype)
            attn_ref[p0 + r] = mixed
            totals.append(jnp.sum(mixed.astype(jnp.float32) * weight, axis=0, keepdims=True))
        part_ref[pl.ds(p0, BATCH), :] = jnp.concatenate(totals, axis=0)
        return carry

    lax.fori_loop(0, rows // BATCH, step, 0)
    pltpu.make_async_copy(buf, buf, out_sem).wait()


def attend(held, arrive, table, length_now, query, fresh, weight, pool):
    rows = query.shape[0]
    pages = held.shape[1]
    return pl.pallas_call(
        functools.partial(attend_kernel, rows, pages),
        out_shape=(
            jax.ShapeDtypeStruct(pool.shape, pool.dtype),
            jax.ShapeDtypeStruct(query.shape, jnp.bfloat16),
            jax.ShapeDtypeStruct((rows, HEAD_DIM), jnp.float32),
        ),
        in_specs=[pl.BlockSpec(memory_space=pltpu.SMEM)] * 3
        + [pl.BlockSpec(memory_space=pltpu.HBM)]
        + [pl.BlockSpec(memory_space=pltpu.VMEM)] * 3,
        out_specs=(
            pl.BlockSpec(memory_space=pl.ANY),
            pl.BlockSpec(memory_space=pltpu.VMEM),
            pl.BlockSpec(memory_space=pltpu.VMEM),
        ),
        scratch_shapes=[
            pltpu.VMEM((rows,) + held.shape[1:], held.dtype),
            pltpu.SemaphoreType.DMA((rows,)),
            pltpu.SemaphoreType.DMA,
        ],
        compiler_params=pltpu.CompilerParams(vmem_limit_bytes=32 << 20),
        name="attend",
    )(arrive, table, length_now, held, query, fresh, weight)


def weights_kernel(devices, prompts, part_ref, out_ref, mine, landed, send_sem, recv_sem):
    me = lax.axis_index("particle")
    rows = part_ref.shape[0]
    lanes = out_ref.shape[1]
    barrier = pltpu.get_barrier_semaphore()

    def greet(k, carry):
        pl.semaphore_signal(
            barrier, inc=1, device_id={"particle": lax.rem(me + k, devices)},
            device_id_type=pl.DeviceIdType.MESH,
        )
        return carry

    lax.fori_loop(1, devices, greet, 0)
    reward = jnp.sum(part_ref[...].T, axis=0, keepdims=True)
    reward = jnp.concatenate([reward] * (lanes // rows), axis=1)
    reward = jnp.broadcast_to(reward, out_ref.shape)
    mine[...] = reward
    pl.semaphore_wait(barrier, devices - 1)

    def copy_to(k):
        return pltpu.make_async_remote_copy(
            src_ref=mine,
            dst_ref=landed.at[k],
            send_sem=send_sem.at[k],
            recv_sem=recv_sem.at[k],
            device_id={"particle": lax.rem(me + k, devices)},
            device_id_type=pl.DeviceIdType.MESH,
        )

    def send(k, carry):
        copy_to(k).start()
        return carry

    def finish(k, carry):
        copy_to(k).wait()
        return carry

    lax.fori_loop(1, devices, send, 0)
    lax.fori_loop(1, devices, finish, 0)
    stride = max(1, prompts // rows)
    table = [reward] + [landed[k] for k in range(stride, devices, stride)]
    shifts = []
    shift = prompts
    while shift < rows:
        shifts.append(shift)
        shift *= 2
    high = functools.reduce(jnp.maximum, table)
    for shift in shifts:
        high = jnp.maximum(high, pltpu.roll(high, shift, 1))
    total = sum(jnp.exp(entry - high) for entry in table)
    for shift in shifts:
        total = total + pltpu.roll(total, shift, 1)
    out_ref[...] = reward - (high + jnp.log(total))


def weights(partial_sums, devices, prompts):
    tile = (8, 128)
    return pl.pallas_call(
        functools.partial(weights_kernel, devices, prompts),
        out_shape=jax.ShapeDtypeStruct(tile, jnp.float32),
        in_specs=[pl.BlockSpec(memory_space=pltpu.VMEM)],
        out_specs=pl.BlockSpec(memory_space=pltpu.VMEM),
        scratch_shapes=[
            pltpu.VMEM(tile, jnp.float32),
            pltpu.VMEM((devices,) + tile, jnp.float32),
            pltpu.SemaphoreType.DMA((devices,)),
            pltpu.SemaphoreType.DMA((devices,)),
        ],
        compiler_params=pltpu.CompilerParams(collective_id=0, has_side_effects=True),
        name="weights",
    )(partial_sums)


def local(pool, page_table, lengths, ancestors, new_q, new_kv, score_weight):
    devices = lax.axis_size("particle")
    self_index = lax.axis_index("particle")
    per_device = new_q.shape[0]
    page_count = page_table.shape[1]
    prompts = devices * per_device // GROUP
    stride = max(1, prompts // per_device)
    reach_size = devices // stride
    capacity = 2 * per_device // reach_size
    table = page_table.reshape(-1)
    anc_all = ancestors.reshape(devices, per_device)
    anc_dev = anc_all // per_device
    row_order = jnp.arange(per_device, dtype=jnp.int32)
    my_ancestors = lax.dynamic_slice_in_dim(anc_all, self_index, 1, 0)[0]
    my_sources = my_ancestors // per_device
    from_self = anc_dev == self_index
    slot_rank = jnp.cumsum(from_self.astype(jnp.int32), axis=1) - 1
    picked = from_self[:, None, :] & (
        slot_rank[:, None, :] == jnp.arange(capacity, dtype=jnp.int32)[None, :, None]
    )
    source_row = jnp.sum(jnp.where(picked, anc_all[:, None, :] % per_device, 0), axis=2)
    incoming = exchange(pool, table, source_row, page_count)
    incoming = incoming.reshape((devices * capacity,) + incoming.shape[2:])
    earlier = (my_sources[None, :] == my_sources[:, None]) & (
        row_order[None, :] < row_order[:, None]
    )
    arrive_slot = my_sources * capacity + jnp.sum(earlier.astype(jnp.int32), axis=1)
    length_now = lengths[my_ancestors]
    new_pool, attn_out, partial_sums = attend(
        incoming, arrive_slot, table, length_now,
        new_q.reshape(per_device, HEADS, HEAD_DIM),
        new_kv.astype(jnp.float32).reshape(per_device, -1),
        score_weight.reshape(HEADS, HEAD_DIM), pool,
    )
    attn_out = attn_out.reshape(new_q.shape)
    log_weights = weights(partial_sums, devices, prompts)[0, :per_device]
    return (new_pool, attn_out, log_weights)


def solution(mesh):
    in_specs = (
        P(("groups", "particle"), None, None, None),
        P(("groups", "particle"), None),
        P("groups"),
        P("groups"),
        P(("groups", "particle"), None),
        P(("groups", "particle"), None, None),
        P(),
    )
    out_specs = (
        P(("groups", "particle"), None, None, None),
        P(("groups", "particle"), None),
        P(("groups", "particle")),
    )
    return jax.shard_map(local, mesh=mesh, in_specs=in_specs, out_specs=out_specs, check_vma=False)
```

```python
import functools

import jax
import jax.numpy as jnp
from jax import lax
from jax.experimental import pallas as pl
from jax.experimental.pallas import tpu as pltpu
from jax.sharding import PartitionSpec as P

HEADS = 64
KV_HEADS = 8
HEAD_DIM = 128
GROUP = 64
BATCH = 16


def exchange_kernel(
    devices, capacity, pages, row_ref, table_ref, pool_ref, held_ref,
    cache, stage, send_sem, recv_sem, own_sem, pool_sem,
):
    me = lax.axis_index("particle")
    half = devices // 2
    own_half = me // half
    place = lax.rem(me, half)
    fetch = pltpu.make_async_copy(pool_ref, cache, pool_sem)
    fetch.start()
    barrier = pltpu.get_barrier_semaphore()

    def greet(k, carry):
        pl.semaphore_signal(
            barrier, inc=1, device_id={"particle": lax.rem(me + k, devices)},
            device_id_type=pl.DeviceIdType.MESH,
        )
        return carry

    lax.fori_loop(1, devices, greet, 0)

    def target(far, j):
        return lax.rem(own_half + far, 2) * half + lax.rem(place + j, half)

    def source(far, j):
        return lax.rem(own_half + far, 2) * half + lax.rem(place + half - j, half)

    def fill(far, j):
        base = target(far, j) * capacity
        for c in range(capacity):
            row = row_ref[base + c]
            for i in range(pages):
                stage[far * half + j, c, i] = cache[table_ref[row * pages + i]]

    def copy(far, j, block):
        k = far * half + j
        return pltpu.make_async_remote_copy(
            src_ref=stage.at[k],
            dst_ref=held_ref.at[block],
            send_sem=send_sem.at[k],
            recv_sem=recv_sem.at[k],
            device_id={"particle": target(far, j)},
            device_id_type=pl.DeviceIdType.MESH,
        )

    def send(far, j):
        fill(far, j)
        copy(far, j, me).start()

    def both(q, carry):
        send(1, 2 * q)
        send(1, 2 * q + 1)
        send(0, q + 1)
        return carry

    def rest(j, carry):
        send(0, j)
        return carry

    def finish_far(j, carry):
        copy(1, j, source(1, j)).wait()
        return carry

    def finish_near(j, carry):
        copy(0, j, source(0, j)).wait()
        return carry

    fetch.wait()
    pl.semaphore_wait(barrier, devices - 1)
    lax.fori_loop(0, half // 2, both, 0)
    lax.fori_loop(half // 2 + 1, half, rest, 0)
    fill(0, 0)
    own = pltpu.make_async_copy(stage.at[0], held_ref.at[me], own_sem)
    own.start()
    lax.fori_loop(1, half, finish_near, 0)
    lax.fori_loop(0, half, finish_far, 0)
    own.wait()


def exchange(pool, table, source_row, pages):
    devices, capacity = source_row.shape
    block = (capacity, pages) + pool.shape[1:]
    return pl.pallas_call(
        functools.partial(exchange_kernel, devices, capacity, pages),
        out_shape=jax.ShapeDtypeStruct((devices,) + block, pool.dtype),
        in_specs=[
            pl.BlockSpec(memory_space=pltpu.SMEM),
            pl.BlockSpec(memory_space=pltpu.SMEM),
            pl.BlockSpec(memory_space=pltpu.HBM),
        ],
        out_specs=pl.BlockSpec(memory_space=pltpu.HBM),
        scratch_shapes=[
            pltpu.VMEM(pool.shape, pool.dtype),
            pltpu.VMEM((devices,) + block, pool.dtype),
            pltpu.SemaphoreType.DMA((devices,)),
            pltpu.SemaphoreType.DMA((devices,)),
            pltpu.SemaphoreType.DMA,
            pltpu.SemaphoreType.DMA,
        ],
        compiler_params=pltpu.CompilerParams(
            collective_id=1, has_side_effects=True, vmem_limit_bytes=58 << 20
        ),
        name="exchange",
    )(source_row.reshape(-1), table, pool)


def attend_kernel(
    rows, pages, arrive_ref, table_ref, len_ref,
    held_ref, q_ref, kv_ref, weight_ref,
    pool_ref, attn_ref, part_ref,
    buf, in_sem, out_sem,
):
    page_len = buf.shape[3]
    width = buf.shape[4]
    ctx = pages * page_len

    def fetch(p, carry):
        pltpu.make_async_copy(held_ref.at[arrive_ref[p]], buf.at[p], in_sem.at[p]).start()
        return carry

    lax.fori_loop(0, rows, fetch, 0, unroll=4)

    cols = KV_HEADS * ctx
    head = lax.broadcasted_iota(jnp.int32, (HEADS, cols), 0) // (HEADS // KV_HEADS)
    col = lax.broadcasted_iota(jnp.int32, (HEADS, cols), 1)
    place = jnp.where(head == col // ctx, col % ctx, ctx)
    row = lax.broadcasted_iota(jnp.int32, (page_len, width), 0)

    def step(b, carry):
        p0 = pl.multiple_of(b * BATCH, BATCH)
        fresh = kv_ref[pl.ds(p0, BATCH), :]
        scores = []
        values = []
        for r in range(BATCH):
            p = p0 + r
            pltpu.make_async_copy(held_ref.at[0], buf.at[p], in_sem.at[p]).wait()
            length = len_ref[p]
            cache = []
            for s in range(2):
                new_row = fresh[r:r + 1, s * width:(s + 1) * width]
                now = []
                for i in range(pages):
                    old = buf[p, i, s].astype(jnp.float32)
                    made = jnp.where(row + i * page_len == length, new_row, old)
                    buf[p, i, s] = made.astype(buf.dtype)
                    now.append(made)
                cache.append(jnp.concatenate(
                    [now[i][:, g * HEAD_DIM:(g + 1) * HEAD_DIM] for g in range(KV_HEADS) for i in range(pages)],
                    axis=0,
                ).astype(jnp.bfloat16))
            for i in range(pages):
                slot = table_ref[p * pages + i]
                pltpu.make_async_copy(buf.at[p, i], pool_ref.at[slot], out_sem).start()
            logits = lax.dot_general(
                q_ref[p], cache[0], (((1,), (1,)), ((), ())), preferred_element_type=jnp.float32
            )
            scores.append(jnp.where(place <= length, logits * HEAD_DIM ** (-0.5), -1e30))
            values.append(cache[1])
        weight = weight_ref[...]
        totals = []
        for r in range(BATCH):
            high = jnp.max(scores[r], axis=1, keepdims=True)
            expo = jnp.exp(scores[r] - high)
            probs = (expo / jnp.sum(expo, axis=1, keepdims=True)).astype(jnp.bfloat16)
            mixed = jnp.dot(probs, values[r], preferred_element_type=jnp.float32).astype(attn_ref.dtype)
            attn_ref[p0 + r] = mixed
            totals.append(jnp.sum(mixed.astype(jnp.float32) * weight, axis=0, keepdims=True))
        part_ref[pl.ds(p0, BATCH), :] = jnp.concatenate(totals, axis=0)
        return carry

    lax.fori_loop(0, rows // BATCH, step, 0)
    pltpu.make_async_copy(buf, buf, out_sem).wait()


def attend(held, arrive, table, length_now, query, fresh, weight, pool):
    rows = query.shape[0]
    pages = held.shape[1]
    return pl.pallas_call(
        functools.partial(attend_kernel, rows, pages),
        out_shape=(
            jax.ShapeDtypeStruct(pool.shape, pool.dtype),
            jax.ShapeDtypeStruct(query.shape, jnp.bfloat16),
            jax.ShapeDtypeStruct((rows, HEAD_DIM), jnp.float32),
        ),
        in_specs=[pl.BlockSpec(memory_space=pltpu.SMEM)] * 3
        + [pl.BlockSpec(memory_space=pltpu.HBM)]
        + [pl.BlockSpec(memory_space=pltpu.VMEM)] * 3,
        out_specs=(
            pl.BlockSpec(memory_space=pl.ANY),
            pl.BlockSpec(memory_space=pltpu.VMEM),
            pl.BlockSpec(memory_space=pltpu.VMEM),
        ),
        scratch_shapes=[
            pltpu.VMEM((rows,) + held.shape[1:], held.dtype),
            pltpu.SemaphoreType.DMA((rows,)),
            pltpu.SemaphoreType.DMA,
        ],
        compiler_params=pltpu.CompilerParams(vmem_limit_bytes=58 << 20),
        name="attend",
    )(arrive, table, length_now, held, query, fresh, weight)


def weights_kernel(devices, prompts, part_ref, out_ref, mine, landed, send_sem, recv_sem):
    me = lax.axis_index("particle")
    rows = part_ref.shape[0]
    lanes = out_ref.shape[1]
    barrier = pltpu.get_barrier_semaphore()

    def greet(k, carry):
        pl.semaphore_signal(
            barrier, inc=1, device_id={"particle": lax.rem(me + k, devices)},
            device_id_type=pl.DeviceIdType.MESH,
        )
        return carry

    lax.fori_loop(1, devices, greet, 0)
    reward = jnp.sum(part_ref[...].T, axis=0, keepdims=True)
    reward = jnp.concatenate([reward] * (lanes // rows), axis=1)
    reward = jnp.broadcast_to(reward, out_ref.shape)
    mine[...] = reward
    pl.semaphore_wait(barrier, devices - 1)

    def copy_to(k):
        return pltpu.make_async_remote_copy(
            src_ref=mine,
            dst_ref=landed.at[k],
            send_sem=send_sem.at[k],
            recv_sem=recv_sem.at[k],
            device_id={"particle": lax.rem(me + k, devices)},
            device_id_type=pl.DeviceIdType.MESH,
        )

    def send(k, carry):
        copy_to(k).start()
        return carry

    def finish(k, carry):
        copy_to(k).wait()
        return carry

    lax.fori_loop(1, devices, send, 0)
    lax.fori_loop(1, devices, finish, 0)
    stride = max(1, prompts // rows)
    table = [reward] + [landed[k] for k in range(stride, devices, stride)]
    shifts = []
    shift = prompts
    while shift < rows:
        shifts.append(shift)
        shift *= 2
    high = functools.reduce(jnp.maximum, table)
    for shift in shifts:
        high = jnp.maximum(high, pltpu.roll(high, shift, 1))
    total = sum(jnp.exp(entry - high) for entry in table)
    for shift in shifts:
        total = total + pltpu.roll(total, shift, 1)
    out_ref[...] = reward - (high + jnp.log(total))


def weights(partial_sums, devices, prompts):
    tile = (8, 128)
    return pl.pallas_call(
        functools.partial(weights_kernel, devices, prompts),
        out_shape=jax.ShapeDtypeStruct(tile, jnp.float32),
        in_specs=[pl.BlockSpec(memory_space=pltpu.VMEM)],
        out_specs=pl.BlockSpec(memory_space=pltpu.VMEM),
        scratch_shapes=[
            pltpu.VMEM(tile, jnp.float32),
            pltpu.VMEM((devices,) + tile, jnp.float32),
            pltpu.SemaphoreType.DMA((devices,)),
            pltpu.SemaphoreType.DMA((devices,)),
        ],
        compiler_params=pltpu.CompilerParams(collective_id=0, has_side_effects=True),
        name="weights",
    )(partial_sums)


def local(pool, page_table, lengths, ancestors, new_q, new_kv, score_weight):
    devices = lax.axis_size("particle")
    self_index = lax.axis_index("particle")
    per_device = new_q.shape[0]
    page_count = page_table.shape[1]
    prompts = devices * per_device // GROUP
    stride = max(1, prompts // per_device)
    reach_size = devices // stride
    capacity = 2 * per_device // reach_size
    table = page_table.reshape(-1)
    anc_all = ancestors.reshape(devices, per_device)
    anc_dev = anc_all // per_device
    row_order = jnp.arange(per_device, dtype=jnp.int32)
    my_ancestors = lax.dynamic_slice_in_dim(anc_all, self_index, 1, 0)[0]
    my_sources = my_ancestors // per_device
    from_self = anc_dev == self_index
    slot_rank = jnp.cumsum(from_self.astype(jnp.int32), axis=1) - 1
    picked = from_self[:, None, :] & (
        slot_rank[:, None, :] == jnp.arange(capacity, dtype=jnp.int32)[None, :, None]
    )
    source_row = jnp.sum(jnp.where(picked, anc_all[:, None, :] % per_device, 0), axis=2)
    incoming = exchange(pool, table, source_row, page_count)
    incoming = incoming.reshape((devices * capacity,) + incoming.shape[2:])
    earlier = (my_sources[None, :] == my_sources[:, None]) & (
        row_order[None, :] < row_order[:, None]
    )
    arrive_slot = my_sources * capacity + jnp.sum(earlier.astype(jnp.int32), axis=1)
    length_now = lengths[my_ancestors]
    new_pool, attn_out, partial_sums = attend(
        incoming, arrive_slot, table, length_now,
        new_q.reshape(per_device, HEADS, HEAD_DIM),
        new_kv.astype(jnp.float32).reshape(per_device, -1),
        score_weight.reshape(HEADS, HEAD_DIM), pool,
    )
    attn_out = attn_out.reshape(new_q.shape)
    log_weights = weights(partial_sums, devices, prompts)[0, :per_device]
    return (new_pool, attn_out, log_weights)


def solution(mesh):
    in_specs = (
        P(("groups", "particle"), None, None, None),
        P(("groups", "particle"), None),
        P("groups"),
        P("groups"),
        P(("groups", "particle"), None),
        P(("groups", "particle"), None, None),
        P(),
    )
    out_specs = (
        P(("groups", "particle"), None, None, None),
        P(("groups", "particle"), None),
        P(("groups", "particle")),
    )
    return jax.shard_map(local, mesh=mesh, in_specs=in_specs, out_specs=out_specs, check_vma=False)
```

```python
import functools

import jax
import jax.numpy as jnp
from jax import lax
from jax.experimental import pallas as pl
from jax.experimental.pallas import tpu as pltpu
from jax.sharding import PartitionSpec as P

HEADS = 64
KV_HEADS = 8
HEAD_DIM = 128
GROUP = 64
BATCH = 8


def exchange_kernel(
    devices, capacity, pages, row_ref, table_ref, pool_ref, held_ref,
    stage, send_sem, recv_sem, own_sem,
):
    me = lax.axis_index("particle")
    barrier = pltpu.get_barrier_semaphore()

    def greet(k, carry):
        pl.semaphore_signal(
            barrier, inc=1, device_id={"particle": lax.rem(me + k, devices)},
            device_id_type=pl.DeviceIdType.MESH,
        )
        return carry

    lax.fori_loop(1, devices, greet, 0)

    def fill(k):
        base = lax.rem(me + k, devices) * capacity
        for c in range(capacity):
            row = row_ref[base + c]
            for i in range(pages):
                stage[k, c, i] = pool_ref[table_ref[row * pages + i]]

    def copy_to(k):
        return pltpu.make_async_remote_copy(
            src_ref=stage.at[k],
            dst_ref=held_ref.at[me],
            send_sem=send_sem.at[k],
            recv_sem=recv_sem.at[k],
            device_id={"particle": lax.rem(me + k, devices)},
            device_id_type=pl.DeviceIdType.MESH,
        )

    def send(i, carry):
        half = i // 2
        odd = half % 2
        step = (half + 1) // 2
        far = devices // 2 + step - 2 * step * odd
        near = (1 - odd) * (devices - 1 - half // 2) + odd * (1 + half // 2)
        k = far + (i % 2) * (near - far)
        fill(k)
        copy_to(k).start()
        return carry

    def finish(k, carry):
        source = lax.rem(me + devices - k, devices)
        pltpu.make_async_remote_copy(
            src_ref=stage.at[k],
            dst_ref=held_ref.at[source],
            send_sem=send_sem.at[k],
            recv_sem=recv_sem.at[k],
            device_id={"particle": lax.rem(me + k, devices)},
            device_id_type=pl.DeviceIdType.MESH,
        ).wait()
        return carry

    pl.semaphore_wait(barrier, devices - 1)
    lax.fori_loop(0, devices - 1, send, 0)
    fill(0)
    own = pltpu.make_async_copy(stage.at[0], held_ref.at[me], own_sem)
    own.start()
    lax.fori_loop(1, devices, finish, 0)
    own.wait()


def exchange(pool, table, source_row, pages):
    devices, capacity = source_row.shape
    block = (capacity, pages) + pool.shape[1:]
    return pl.pallas_call(
        functools.partial(exchange_kernel, devices, capacity, pages),
        out_shape=jax.ShapeDtypeStruct((devices,) + block, pool.dtype),
        in_specs=[
            pl.BlockSpec(memory_space=pltpu.SMEM),
            pl.BlockSpec(memory_space=pltpu.SMEM),
            pl.BlockSpec(memory_space=pltpu.VMEM),
        ],
        out_specs=pl.BlockSpec(memory_space=pltpu.HBM),
        scratch_shapes=[
            pltpu.VMEM((devices,) + block, pool.dtype),
            pltpu.SemaphoreType.DMA((devices,)),
            pltpu.SemaphoreType.DMA((devices,)),
            pltpu.SemaphoreType.DMA,
        ],
        compiler_params=pltpu.CompilerParams(
            collective_id=1, has_side_effects=True, vmem_limit_bytes=48 << 20
        ),
        name="exchange",
    )(source_row.reshape(-1), table, pool)


def attend_kernel(
    rows, pages, arrive_ref, table_ref, len_ref,
    held_ref, q_ref, kv_ref, weight_ref,
    pool_ref, attn_ref, part_ref,
    buf, in_sem, out_sem,
):
    page_len = buf.shape[3]
    width = buf.shape[4]
    ctx = pages * page_len

    def fetch(p, carry):
        pltpu.make_async_copy(held_ref.at[arrive_ref[p]], buf.at[p], in_sem.at[p]).start()
        return carry

    lax.fori_loop(0, rows, fetch, 0, unroll=4)

    cols = KV_HEADS * ctx
    head = lax.broadcasted_iota(jnp.int32, (HEADS, cols), 0) // (HEADS // KV_HEADS)
    col = lax.broadcasted_iota(jnp.int32, (HEADS, cols), 1)
    place = jnp.where(head == col // ctx, col % ctx, ctx)
    row = lax.broadcasted_iota(jnp.int32, (page_len, width), 0)

    def step(b, carry):
        p0 = pl.multiple_of(b * BATCH, BATCH)
        fresh = kv_ref[pl.ds(p0, BATCH), :]
        scores = []
        values = []
        for r in range(BATCH):
            p = p0 + r
            pltpu.make_async_copy(held_ref.at[0], buf.at[p], in_sem.at[p]).wait()
            length = len_ref[p]
            cache = []
            for s in range(2):
                new_row = fresh[r:r + 1, s * width:(s + 1) * width]
                now = []
                for i in range(pages):
                    old = buf[p, i, s].astype(jnp.float32)
                    made = jnp.where(row + i * page_len == length, new_row, old)
                    buf[p, i, s] = made.astype(buf.dtype)
                    now.append(made)
                cache.append(jnp.concatenate(
                    [now[i][:, g * HEAD_DIM:(g + 1) * HEAD_DIM] for g in range(KV_HEADS) for i in range(pages)],
                    axis=0,
                ).astype(jnp.bfloat16))
            for i in range(pages):
                slot = table_ref[p * pages + i]
                pltpu.make_async_copy(buf.at[p, i], pool_ref.at[slot], out_sem).start()
            logits = lax.dot_general(
                q_ref[p], cache[0], (((1,), (1,)), ((), ())), preferred_element_type=jnp.float32
            )
            scores.append(jnp.where(place <= length, logits * HEAD_DIM ** (-0.5), -1e30))
            values.append(cache[1])
        weight = weight_ref[...]
        totals = []
        for r in range(BATCH):
            high = jnp.max(scores[r], axis=1, keepdims=True)
            expo = jnp.exp(scores[r] - high)
            probs = (expo / jnp.sum(expo, axis=1, keepdims=True)).astype(jnp.bfloat16)
            mixed = jnp.dot(probs, values[r], preferred_element_type=jnp.float32).astype(attn_ref.dtype)
            attn_ref[p0 + r] = mixed
            totals.append(jnp.sum(mixed.astype(jnp.float32) * weight, axis=0, keepdims=True))
        part_ref[pl.ds(p0, BATCH), :] = jnp.concatenate(totals, axis=0)
        return carry

    lax.fori_loop(0, rows // BATCH, step, 0)
    pltpu.make_async_copy(buf, buf, out_sem).wait()


def attend(held, arrive, table, length_now, query, fresh, weight, pool):
    rows = query.shape[0]
    pages = held.shape[1]
    return pl.pallas_call(
        functools.partial(attend_kernel, rows, pages),
        out_shape=(
            jax.ShapeDtypeStruct(pool.shape, pool.dtype),
            jax.ShapeDtypeStruct(query.shape, jnp.bfloat16),
            jax.ShapeDtypeStruct((rows, HEAD_DIM), jnp.float32),
        ),
        in_specs=[pl.BlockSpec(memory_space=pltpu.SMEM)] * 3
        + [pl.BlockSpec(memory_space=pltpu.HBM)]
        + [pl.BlockSpec(memory_space=pltpu.VMEM)] * 3,
        out_specs=(
            pl.BlockSpec(memory_space=pl.ANY),
            pl.BlockSpec(memory_space=pltpu.VMEM),
            pl.BlockSpec(memory_space=pltpu.VMEM),
        ),
        scratch_shapes=[
            pltpu.VMEM((rows,) + held.shape[1:], held.dtype),
            pltpu.SemaphoreType.DMA((rows,)),
            pltpu.SemaphoreType.DMA,
        ],
        compiler_params=pltpu.CompilerParams(vmem_limit_bytes=52 << 20),
        name="attend",
    )(arrive, table, length_now, held, query, fresh, weight)


def weights_kernel(devices, prompts, part_ref, out_ref, mine, landed, send_sem, recv_sem):
    me = lax.axis_index("particle")
    rows = part_ref.shape[0]
    lanes = out_ref.shape[1]
    barrier = pltpu.get_barrier_semaphore()

    def greet(k, carry):
        pl.semaphore_signal(
            barrier, inc=1, device_id={"particle": lax.rem(me + k, devices)},
            device_id_type=pl.DeviceIdType.MESH,
        )
        return carry

    lax.fori_loop(1, devices, greet, 0)
    reward = jnp.sum(part_ref[...].T, axis=0, keepdims=True)
    reward = jnp.concatenate([reward] * (lanes // rows), axis=1)
    reward = jnp.broadcast_to(reward, out_ref.shape)
    mine[...] = reward
    pl.semaphore_wait(barrier, devices - 1)

    def copy_to(k):
        return pltpu.make_async_remote_copy(
            src_ref=mine,
            dst_ref=landed.at[k],
            send_sem=send_sem.at[k],
            recv_sem=recv_sem.at[k],
            device_id={"particle": lax.rem(me + k, devices)},
            device_id_type=pl.DeviceIdType.MESH,
        )

    def send(k, carry):
        copy_to(k).start()
        return carry

    def finish(k, carry):
        copy_to(k).wait()
        return carry

    lax.fori_loop(1, devices, send, 0)
    lax.fori_loop(1, devices, finish, 0)
    stride = max(1, prompts // rows)
    table = [reward] + [landed[k] for k in range(stride, devices, stride)]
    shifts = []
    shift = prompts
    while shift < rows:
        shifts.append(shift)
        shift *= 2
    high = functools.reduce(jnp.maximum, table)
    for shift in shifts:
        high = jnp.maximum(high, pltpu.roll(high, shift, 1))
    total = sum(jnp.exp(entry - high) for entry in table)
    for shift in shifts:
        total = total + pltpu.roll(total, shift, 1)
    out_ref[...] = reward - (high + jnp.log(total))


def weights(partial_sums, devices, prompts):
    tile = (8, 128)
    return pl.pallas_call(
        functools.partial(weights_kernel, devices, prompts),
        out_shape=jax.ShapeDtypeStruct(tile, jnp.float32),
        in_specs=[pl.BlockSpec(memory_space=pltpu.VMEM)],
        out_specs=pl.BlockSpec(memory_space=pltpu.VMEM),
        scratch_shapes=[
            pltpu.VMEM(tile, jnp.float32),
            pltpu.VMEM((devices,) + tile, jnp.float32),
            pltpu.SemaphoreType.DMA((devices,)),
            pltpu.SemaphoreType.DMA((devices,)),
        ],
        compiler_params=pltpu.CompilerParams(collective_id=0, has_side_effects=True),
        name="weights",
    )(partial_sums)


def local(pool, page_table, lengths, ancestors, new_q, new_kv, score_weight):
    devices = lax.axis_size("particle")
    self_index = lax.axis_index("particle")
    per_device = new_q.shape[0]
    page_count = page_table.shape[1]
    prompts = devices * per_device // GROUP
    stride = max(1, prompts // per_device)
    reach_size = devices // stride
    capacity = 2 * per_device // reach_size
    table = page_table.reshape(-1)
    anc_all = ancestors.reshape(devices, per_device)
    anc_dev = anc_all // per_device
    row_order = jnp.arange(per_device, dtype=jnp.int32)
    my_ancestors = lax.dynamic_slice_in_dim(anc_all, self_index, 1, 0)[0]
    my_sources = my_ancestors // per_device
    from_self = anc_dev == self_index
    slot_rank = jnp.cumsum(from_self.astype(jnp.int32), axis=1) - 1
    picked = from_self[:, None, :] & (
        slot_rank[:, None, :] == jnp.arange(capacity, dtype=jnp.int32)[None, :, None]
    )
    source_row = jnp.sum(jnp.where(picked, anc_all[:, None, :] % per_device, 0), axis=2)
    incoming = exchange(pool, table, source_row, page_count)
    incoming = incoming.reshape((devices * capacity,) + incoming.shape[2:])
    earlier = (my_sources[None, :] == my_sources[:, None]) & (
        row_order[None, :] < row_order[:, None]
    )
    arrive_slot = my_sources * capacity + jnp.sum(earlier.astype(jnp.int32), axis=1)
    length_now = lengths[my_ancestors]
    new_pool, attn_out, partial_sums = attend(
        incoming, arrive_slot, table, length_now,
        new_q.reshape(per_device, HEADS, HEAD_DIM),
        new_kv.astype(jnp.float32).reshape(per_device, -1),
        score_weight.reshape(HEADS, HEAD_DIM), pool,
    )
    attn_out = attn_out.reshape(new_q.shape)
    log_weights = weights(partial_sums, devices, prompts)[0, :per_device]
    return (new_pool, attn_out, log_weights)


def solution(mesh):
    in_specs = (
        P(("groups", "particle"), None, None, None),
        P(("groups", "particle"), None),
        P("groups"),
        P("groups"),
        P(("groups", "particle"), None),
        P(("groups", "particle"), None, None),
        P(),
    )
    out_specs = (
        P(("groups", "particle"), None, None, None),
        P(("groups", "particle"), None),
        P(("groups", "particle")),
    )
    return jax.shard_map(local, mesh=mesh, in_specs=in_specs, out_specs=out_specs, check_vma=False)
```

```python
import functools

import jax
import jax.numpy as jnp
from jax import lax
from jax.experimental import pallas as pl
from jax.experimental.pallas import tpu as pltpu
from jax.sharding import PartitionSpec as P

HEADS = 64
KV_HEADS = 8
HEAD_DIM = 128
GROUP = 64
BATCH = 8


def exchange_kernel(
    devices, capacity, pages, row_ref, table_ref, pool_ref, held_ref,
    stage, send_sem, recv_sem, own_sem,
):
    me = lax.axis_index("particle")
    barrier = pltpu.get_barrier_semaphore()

    def greet(k, carry):
        pl.semaphore_signal(
            barrier, inc=1, device_id={"particle": lax.rem(me + k, devices)},
            device_id_type=pl.DeviceIdType.MESH,
        )
        return carry

    lax.fori_loop(1, devices, greet, 0)

    def fill(k):
        base = lax.rem(me + k, devices) * capacity
        for c in range(capacity):
            row = row_ref[base + c]
            for i in range(pages):
                stage[k, c, i] = pool_ref[table_ref[row * pages + i]]

    def copy_to(k):
        return pltpu.make_async_remote_copy(
            src_ref=stage.at[k],
            dst_ref=held_ref.at[me],
            send_sem=send_sem.at[k],
            recv_sem=recv_sem.at[k],
            device_id={"particle": lax.rem(me + k, devices)},
            device_id_type=pl.DeviceIdType.MESH,
        )

    def send(i, carry):
        half = i // 2
        odd = half % 2
        step = (half + 1) // 2
        far = devices // 2 + step - 2 * step * odd
        near = (1 - odd) * (devices - 1 - half // 2) + odd * (1 + half // 2)
        k = far + (i % 2) * (near - far)
        fill(k)
        copy_to(k).start()
        return carry

    def finish(k, carry):
        source = lax.rem(me + devices - k, devices)
        pltpu.make_async_remote_copy(
            src_ref=stage.at[k],
            dst_ref=held_ref.at[source],
            send_sem=send_sem.at[k],
            recv_sem=recv_sem.at[k],
            device_id={"particle": lax.rem(me + k, devices)},
            device_id_type=pl.DeviceIdType.MESH,
        ).wait()
        return carry

    pl.semaphore_wait(barrier, devices - 1)
    lax.fori_loop(0, devices - 1, send, 0)
    fill(0)
    own = pltpu.make_async_copy(stage.at[0], held_ref.at[me], own_sem)
    own.start()
    lax.fori_loop(1, devices, finish, 0)
    own.wait()


def exchange(pool, table, source_row, pages):
    devices, capacity = source_row.shape
    block = (capacity, pages) + pool.shape[1:]
    return pl.pallas_call(
        functools.partial(exchange_kernel, devices, capacity, pages),
        out_shape=jax.ShapeDtypeStruct((devices,) + block, pool.dtype),
        in_specs=[
            pl.BlockSpec(memory_space=pltpu.SMEM),
            pl.BlockSpec(memory_space=pltpu.SMEM),
            pl.BlockSpec(memory_space=pltpu.VMEM),
        ],
        out_specs=pl.BlockSpec(memory_space=pltpu.HBM),
        scratch_shapes=[
            pltpu.VMEM((devices,) + block, pool.dtype),
            pltpu.SemaphoreType.DMA((devices,)),
            pltpu.SemaphoreType.DMA((devices,)),
            pltpu.SemaphoreType.DMA,
        ],
        compiler_params=pltpu.CompilerParams(
            collective_id=1, has_side_effects=True, vmem_limit_bytes=48 << 20
        ),
        name="exchange",
    )(source_row.reshape(-1), table, pool)


def attend_kernel(
    rows, pages, arrive_ref, table_ref, len_ref,
    held_ref, q_ref, kv_ref, weight_ref,
    pool_ref, attn_ref, part_ref,
    buf, in_sem, out_sem,
):
    page_len = buf.shape[3]
    width = buf.shape[4]
    ctx = pages * page_len

    def fetch(p, carry):
        pltpu.make_async_copy(held_ref.at[arrive_ref[p]], buf.at[p], in_sem.at[p]).start()
        return carry

    lax.fori_loop(0, rows, fetch, 0, unroll=4)

    cols = KV_HEADS * ctx
    head = lax.broadcasted_iota(jnp.int32, (HEADS, cols), 0) // (HEADS // KV_HEADS)
    col = lax.broadcasted_iota(jnp.int32, (HEADS, cols), 1)
    place = jnp.where(head == col // ctx, col % ctx, ctx)
    row = lax.broadcasted_iota(jnp.int32, (page_len, width), 0)

    def step(b, carry):
        p0 = pl.multiple_of(b * BATCH, BATCH)
        fresh = kv_ref[pl.ds(p0, BATCH), :]
        scores = []
        values = []
        for r in range(BATCH):
            p = p0 + r
            pltpu.make_async_copy(held_ref.at[0], buf.at[p], in_sem.at[p]).wait()
            length = len_ref[p]
            cache = []
            for s in range(2):
                new_row = fresh[r:r + 1, s * width:(s + 1) * width]
                now = []
                for i in range(pages):
                    old = buf[p, i, s].astype(jnp.float32)
                    made = jnp.where(row + i * page_len == length, new_row, old)
                    buf[p, i, s] = made.astype(buf.dtype)
                    now.append(made)
                cache.append(jnp.concatenate(
                    [now[i][:, g * HEAD_DIM:(g + 1) * HEAD_DIM] for g in range(KV_HEADS) for i in range(pages)],
                    axis=0,
                ).astype(jnp.bfloat16))
            for i in range(pages):
                slot = table_ref[p * pages + i]
                pltpu.make_async_copy(buf.at[p, i], pool_ref.at[slot], out_sem).start()
            logits = lax.dot_general(
                q_ref[p], cache[0], (((1,), (1,)), ((), ())), preferred_element_type=jnp.float32
            )
            scores.append(jnp.where(place <= length, logits * HEAD_DIM ** (-0.5), -1e30))
            values.append(cache[1])
        weight = weight_ref[...]
        totals = []
        for r in range(BATCH):
            high = jnp.max(scores[r], axis=1, keepdims=True)
            expo = jnp.exp(scores[r] - high)
            probs = (expo / jnp.sum(expo, axis=1, keepdims=True)).astype(jnp.bfloat16)
            mixed = jnp.dot(probs, values[r], preferred_element_type=jnp.float32).astype(attn_ref.dtype)
            attn_ref[p0 + r] = mixed
            totals.append(jnp.sum(mixed.astype(jnp.float32) * weight, axis=0, keepdims=True))
        part_ref[pl.ds(p0, BATCH), :] = jnp.concatenate(totals, axis=0)
        return carry

    lax.fori_loop(0, rows // BATCH, step, 0)
    pltpu.make_async_copy(buf, buf, out_sem).wait()


def attend(held, arrive, table, length_now, query, fresh, weight, pool):
    rows = query.shape[0]
    pages = held.shape[1]
    return pl.pallas_call(
        functools.partial(attend_kernel, rows, pages),
        out_shape=(
            jax.ShapeDtypeStruct(pool.shape, pool.dtype),
            jax.ShapeDtypeStruct(query.shape, jnp.bfloat16),
            jax.ShapeDtypeStruct((rows, HEAD_DIM), jnp.float32),
        ),
        in_specs=[pl.BlockSpec(memory_space=pltpu.SMEM)] * 3
        + [pl.BlockSpec(memory_space=pltpu.HBM)]
        + [pl.BlockSpec(memory_space=pltpu.VMEM)] * 3,
        out_specs=(
            pl.BlockSpec(memory_space=pl.ANY),
            pl.BlockSpec(memory_space=pltpu.VMEM),
            pl.BlockSpec(memory_space=pltpu.VMEM),
        ),
        scratch_shapes=[
            pltpu.VMEM((rows,) + held.shape[1:], held.dtype),
            pltpu.SemaphoreType.DMA((rows,)),
            pltpu.SemaphoreType.DMA,
        ],
        compiler_params=pltpu.CompilerParams(vmem_limit_bytes=52 << 20),
        name="attend",
    )(arrive, table, length_now, held, query, fresh, weight)


def weights_kernel(devices, prompts, part_ref, out_ref, mine, landed, send_sem, recv_sem):
    me = lax.axis_index("particle")
    rows = part_ref.shape[0]
    lanes = out_ref.shape[1]
    barrier = pltpu.get_barrier_semaphore()

    def greet(k, carry):
        pl.semaphore_signal(
            barrier, inc=1, device_id={"particle": lax.rem(me + k, devices)},
            device_id_type=pl.DeviceIdType.MESH,
        )
        return carry

    lax.fori_loop(1, devices, greet, 0)
    reward = jnp.sum(part_ref[...].T, axis=0, keepdims=True)
    reward = jnp.concatenate([reward] * (lanes // rows), axis=1)
    reward = jnp.broadcast_to(reward, out_ref.shape)
    mine[...] = reward
    pl.semaphore_wait(barrier, devices - 1)

    def copy_to(k):
        return pltpu.make_async_remote_copy(
            src_ref=mine,
            dst_ref=landed.at[k],
            send_sem=send_sem.at[k],
            recv_sem=recv_sem.at[k],
            device_id={"particle": lax.rem(me + k, devices)},
            device_id_type=pl.DeviceIdType.MESH,
        )

    def send(k, carry):
        copy_to(k).start()
        return carry

    def finish(k, carry):
        copy_to(k).wait()
        return carry

    lax.fori_loop(1, devices, send, 0)
    lax.fori_loop(1, devices, finish, 0)
    stride = max(1, prompts // rows)
    table = [reward] + [landed[k] for k in range(stride, devices, stride)]
    shifts = []
    shift = prompts
    while shift < rows:
        shifts.append(shift)
        shift *= 2
    high = functools.reduce(jnp.maximum, table)
    for shift in shifts:
        high = jnp.maximum(high, pltpu.roll(high, shift, 1))
    total = sum(jnp.exp(entry - high) for entry in table)
    for shift in shifts:
        total = total + pltpu.roll(total, shift, 1)
    out_ref[...] = reward - (high + jnp.log(total))


def weights(partial_sums, devices, prompts):
    tile = (8, 128)
    return pl.pallas_call(
        functools.partial(weights_kernel, devices, prompts),
        out_shape=jax.ShapeDtypeStruct(tile, jnp.float32),
        in_specs=[pl.BlockSpec(memory_space=pltpu.VMEM)],
        out_specs=pl.BlockSpec(memory_space=pltpu.VMEM),
        scratch_shapes=[
            pltpu.VMEM(tile, jnp.float32),
            pltpu.VMEM((devices,) + tile, jnp.float32),
            pltpu.SemaphoreType.DMA((devices,)),
            pltpu.SemaphoreType.DMA((devices,)),
        ],
        compiler_params=pltpu.CompilerParams(collective_id=0, has_side_effects=True),
        name="weights",
    )(partial_sums)


def local(pool, page_table, lengths, ancestors, new_q, new_kv, score_weight):
    devices = lax.axis_size("particle")
    self_index = lax.axis_index("particle")
    per_device = new_q.shape[0]
    page_count = page_table.shape[1]
    prompts = devices * per_device // GROUP
    stride = max(1, prompts // per_device)
    reach_size = devices // stride
    capacity = 2 * per_device // reach_size
    table = page_table.reshape(-1)
    anc_all = ancestors.reshape(devices, per_device)
    anc_dev = anc_all // per_device
    row_order = jnp.arange(per_device, dtype=jnp.int32)
    my_ancestors = lax.dynamic_slice_in_dim(anc_all, self_index, 1, 0)[0]
    my_sources = my_ancestors // per_device
    from_self = anc_dev == self_index
    slot_rank = jnp.cumsum(from_self.astype(jnp.int32), axis=1) - 1
    picked = from_self[:, None, :] & (
        slot_rank[:, None, :] == jnp.arange(capacity, dtype=jnp.int32)[None, :, None]
    )
    source_row = jnp.sum(jnp.where(picked, anc_all[:, None, :] % per_device, 0), axis=2)
    incoming = exchange(pool, table, source_row, page_count)
    incoming, new_q, new_kv = lax.optimization_barrier((incoming, new_q, new_kv))
    incoming = incoming.reshape((devices * capacity,) + incoming.shape[2:])
    earlier = (my_sources[None, :] == my_sources[:, None]) & (
        row_order[None, :] < row_order[:, None]
    )
    arrive_slot = my_sources * capacity + jnp.sum(earlier.astype(jnp.int32), axis=1)
    length_now = lengths[my_ancestors]
    new_pool, attn_out, partial_sums = attend(
        incoming, arrive_slot, table, length_now,
        new_q.reshape(per_device, HEADS, HEAD_DIM),
        new_kv.astype(jnp.float32).reshape(per_device, -1),
        score_weight.reshape(HEADS, HEAD_DIM), pool,
    )
    attn_out = attn_out.reshape(new_q.shape)
    log_weights = weights(partial_sums, devices, prompts)[0, :per_device]
    return (new_pool, attn_out, log_weights)


def solution(mesh):
    in_specs = (
        P(("groups", "particle"), None, None, None),
        P(("groups", "particle"), None),
        P("groups"),
        P("groups"),
        P(("groups", "particle"), None),
        P(("groups", "particle"), None, None),
        P(),
    )
    out_specs = (
        P(("groups", "particle"), None, None, None),
        P(("groups", "particle"), None),
        P(("groups", "particle")),
    )
    return jax.shard_map(local, mesh=mesh, in_specs=in_specs, out_specs=out_specs, check_vma=False)
```
